32 devices in a mesh: rec: 2 (over y), tm: 4 (over z), chan: 4 (over x, core).
Axes of the slice: x: 2, y: 2, z: 4, core: 2. Of those that a mesh axis runs over, the one named last changes fastest.
Arguments:
- waveform: bfloat16 [204800], P(('rec', 'tm')), parts along dimension 0, may hold values from -56 to 56, as said below
- first_weight: bfloat16 [10, 512], P(None, 'chan'), may hold values from -2 to 2
- instance_gain: float32 [512], P('chan'), may hold values from 0.5 to 2
- instance_bias: float32 [512], P('chan'), may hold values from -3 to 3
- second_weight: bfloat16 [3, 512, 512], P(None, None, 'chan'), may hold values from -0.15625 to 0.15625
- third_weight: bfloat16 [3, 512, 512], P(None, None, 'chan'), may hold values from -0.15625 to 0.15625
- feature_gain: float32 [512], replicated, may hold values from 0.5 to 2
- feature_bias: float32 [512], replicated, may hold values from -3 to 3
- project_weight: bfloat16 [512, 1024], P(None, 'chan'), may hold values from -0.25 to 0.25
- project_bias: float32 [1024], replicated, may hold values from -3 to 3
- position_weight: bfloat16 [1024, 8192], P('chan'), may hold values from -0.0625 to 0.0625
- position_bias: float32 [1024], P('chan'), may hold values from -3 to 3
- final_gain: float32 [1024], P('chan'), may hold values from 0.5 to 2
- final_bias: float32 [1024], P('chan'), may hold values from -3 to 3
Outputs:
- encoded: bfloat16 [1024, 10240], P('chan', ('rec', 'tm')), parts along dimension 1
The draws below stay inside these ranges and needn't reach their ends.
There are 2 independent parts, one for each index of `rec`. The reference program is written for one: setup_inputs(seed, part) draws one part's arguments, and reference() takes and returns one part's arrays. A program takes and returns all parts, laid end to end along the dimension named above; an argument that names none is the same for every part. Nothing has to cross between parts.
Inputs may be any that keep to these rules, and one draw needn't show every extreme that they name: `waveform`: samples of one recording.
All inputs are finite; a program needn't handle non-finite values.
Results may differ from the reference program's by a relative error of at most 0.005.
The reference program's roundings to bfloat16 on the way (of `first`, `second`, `third`, `normed` and `projected`) count: a program that leaves them out, or rounds other values in their place, can miss the bound.
Values may be sent and summed in bfloat16 or wider, within the bound.
A program may use at most 128 MiB of HBM per device.

```python
import math
import jax
import jax.numpy as jnp
from jax import lax

C = 512
D = 1024
K = 128
GROUPS = 16
GW = 64
SAMPLES = 102400
FRAMES_A = 20480
FRAMES_B = 10240
FRAMES_C = 5120


def draw_waveform(key, part):
    keys = jax.random.split(key, 2)
    position = jnp.arange(SAMPLES, dtype=jnp.float32) / SAMPLES
    jitter = jax.random.uniform(keys[1], (SAMPLES // 320,), jnp.float32, 0.7, 1.4)
    envelope = jnp.exp(jnp.log(10.0) * position) * jnp.repeat(jitter, 320, total_repeat_length=SAMPLES)
    noise = jax.random.truncated_normal(keys[0], -4.0, 4.0, (SAMPLES,), jnp.float32)
    return (noise * envelope).astype(jnp.bfloat16)


def shard_levels(own_key, dims, cuts, low, high):
    def one(dim, blocks):
        draws = jax.random.uniform(jax.random.fold_in(jax.random.fold_in(own_key, 6), dim), (blocks,), jnp.float32, low / len(cuts), high / len(cuts))
        return jnp.repeat(jnp.exp(draws), dims[dim] // blocks).reshape((-1,) + (1,) * (len(dims) - dim - 1))

    level = one(*cuts[0])
    for cut in cuts[1:]:
        level = level * one(*cut)
    return level


def normal_values(rng, shape, scale, limit, pieces=(), held_as=jnp.bfloat16):
    entries = jax.random.normal(rng, shape, jnp.float32) * scale
    if len(pieces) > 0:
        entries = shard_levels(rng, shape, pieces, -0.22, 0.18) * entries
    return jnp.clip(entries, min=-limit, max=limit).astype(held_as)


def setup_inputs(seed: int = 0, part: int = 0) -> dict:
    key_of = jax.random.split(jax.random.key(seed), 15)
    part_keys = jax.random.split(jax.random.fold_in(key_of[14], part), 15)
    return {
        "waveform": draw_waveform(jax.random.fold_in(jax.random.fold_in(key_of[14], part), 71), part),
        "first_weight": normal_values(key_of[1], (10, C), 10 ** -0.5, 2.0, ((1, 4),)),
        "instance_gain": jnp.clip(jnp.exp(math.log(2.0) - 1.3862944 * jax.random.uniform(key_of[2], (C,), jnp.float32) ** shard_levels(key_of[2], (C,), ((0, 4),), -0.2, 0.2)), 0.5, 2.0),
        "instance_bias": normal_values(key_of[3], (C,), 0.5, 3.0, ((0, 4),), jnp.float32),
        "second_weight": normal_values(key_of[4], (3, C, C), (3 * C) ** -0.5, 0.15625, ((2, 4),)),
        "third_weight": normal_values(key_of[5], (3, C, C), (3 * C) ** -0.5, 0.15625, ((2, 4),)),
        "feature_gain": jnp.clip(jnp.exp(jax.random.uniform(key_of[6], (C,), jnp.float32, math.log(0.5), math.log(2.0))), 0.5, 2.0),
        "feature_bias": normal_values(key_of[7], (C,), 0.5, 3.0, (), jnp.float32),
        "project_weight": normal_values(key_of[8], (C, D), C ** -0.5, 0.25, ((1, 4),)),
        "project_bias": normal_values(key_of[9], (D,), 0.5, 3.0, (), jnp.float32),
        "position_weight": normal_values(key_of[10], (D, K * GW), (K * GW) ** -0.5, 0.0625, ((0, 4),)),
        "position_bias": normal_values(key_of[11], (D,), 0.5, 3.0, ((0, 4),), jnp.float32),
        "final_gain": jnp.clip(jnp.exp(math.log(2.0) - 1.3862944 * jax.random.uniform(key_of[12], (D,), jnp.float32) ** shard_levels(key_of[12], (D,), ((0, 4),), -0.2, 0.2)), 0.5, 2.0),
        "final_bias": normal_values(key_of[13], (D,), 0.5, 3.0, ((0, 4),), jnp.float32),
    }


def gelu_exact(values):
    return jax.nn.gelu(values, approximate=False)

def strided_taps(extended, weight, count):
    total = jnp.dot(extended[0:2 * count:2], weight[0], preferred_element_type=jnp.float32)
    total = total + jnp.dot(extended[1:2 * count:2], weight[1], preferred_element_type=jnp.float32)
    total = total + jnp.dot(extended[2:2 * count + 1:2], weight[2], preferred_element_type=jnp.float32)
    return total

def feature_norm(rows, gain, bias):
    values = rows.astype(jnp.float32)
    mean = lax.optimization_barrier(jnp.mean(values, axis=1, keepdims=True))
    centred = values - mean
    spread = lax.optimization_barrier(jnp.mean(centred * centred, axis=1, keepdims=True))
    return (centred * lax.rsqrt(spread + 1e-05) * gain + bias).astype(jnp.bfloat16)

def reference(waveform, first_weight, instance_gain, instance_bias, second_weight, third_weight, feature_gain, feature_bias, project_weight, project_bias, position_weight, position_bias, final_gain, final_bias):
    padded = jnp.concatenate([waveform, jnp.zeros((5,), jnp.bfloat16)])
    blocks = padded.reshape(FRAMES_A + 1, 5)
    patches = jnp.concatenate([blocks[:-1], blocks[1:]], axis=1)
    conv_first = jnp.dot(patches, first_weight, preferred_element_type=jnp.float32)
    mean_first = lax.optimization_barrier(jnp.sum(conv_first, axis=0)) / FRAMES_A
    var_first = lax.optimization_barrier(jnp.sum(conv_first * conv_first, axis=0)) / FRAMES_A - mean_first * mean_first
    first = gelu_exact((conv_first - mean_first) * lax.rsqrt(var_first + 1e-05) * instance_gain + instance_bias).astype(jnp.bfloat16)
    zero_row = jnp.zeros((1, C), jnp.bfloat16)
    second = gelu_exact(strided_taps(jnp.concatenate([first, zero_row], 0), second_weight, FRAMES_B)).astype(jnp.bfloat16)
    third = gelu_exact(strided_taps(jnp.concatenate([second, zero_row], 0), third_weight, FRAMES_C)).astype(jnp.bfloat16)
    normed = feature_norm(third, feature_gain, feature_bias)
    projected = (jnp.dot(normed, project_weight, preferred_element_type=jnp.float32) + project_bias).astype(jnp.bfloat16)
    half = K // 2
    extended = jnp.pad(projected.astype(jnp.float32), ((half, half), (0, 0)))
    grouped = extended.reshape(FRAMES_C + K, GROUPS, GW).transpose(1, 0, 2)
    tap_major = position_weight.astype(jnp.float32).reshape(D, K, GW).transpose(1, 2, 0)
    kernels = tap_major.reshape(K, GW, GROUPS, GW).transpose(2, 0, 1, 3)

    def one_group(pair):
        rows, kernel = pair

        def add_tap(index, total):
            window = lax.dynamic_slice_in_dim(rows, index, FRAMES_C, 0)
            return total + jnp.dot(window, kernel[index], preferred_element_type=jnp.float32)
        return lax.fori_loop(0, K, add_tap, jnp.zeros((FRAMES_C, GW), jnp.float32))
    outputs = lax.map(one_group, (grouped, kernels))
    positional = outputs.transpose(1, 0, 2).reshape(FRAMES_C, D) + position_bias
    summed = projected.astype(jnp.float32) + gelu_exact(positional)
    mean_row = lax.optimization_barrier(jnp.sum(summed, axis=1, keepdims=True)) / D
    square_row = lax.optimization_barrier(jnp.sum(summed * summed, axis=1, keepdims=True)) / D - mean_row * mean_row
    encoded = (summed - mean_row) * lax.rsqrt(square_row + 1e-05) * final_gain + final_bias
    return encoded.astype(jnp.bfloat16).T
```

```python
import functools

import jax
import jax.numpy as jnp
from jax import lax
from jax.experimental import pallas as pl
from jax.experimental.pallas import tpu as pltpu
from jax.sharding import PartitionSpec as P

K = 128
GW = 64
HALF = K // 2
SPAN = 32
PHASES = K // SPAN
MESH = pl.DeviceIdType.MESH
NT = (((1,), (1,)), ((), ()))


def gelu_exact(values):
    return 0.5 * values * (1.0 + lax.erf(values * 0.7071067811865476))


def rows_per_device(frames, count):
    return -(-(frames + K) // (16 * count)) * 16


def shifted(value, axis, steps):
    count = lax.axis_size(axis)
    leading, last = (max(0, -steps), min(count, count - steps))
    return lax.ppermute(value, axis, [(source, source + steps) for source in range(leading, last)])


def tail_kernel(
    n,
    frames,
    rows,
    model_width,
    normed,
    project_weight,
    params,
    position_weight,
    out,
    gathered,
    taps,
    x32,
    x2,
    window,
    partial,
    positional,
    summed,
    stats,
    taps_sem,
    send_sem,
    recv_sem,
    pair_send,
    pair_recv,
    stat_send,
    stat_recv,
):
    me = lax.axis_index("chan")
    shard = lax.axis_index("tm")
    shards = lax.axis_size("tm")
    chips = n // 2
    chip, core = me // 2, lax.rem(me, 2)
    pair = chip * 2 + 1 - core
    width = out.shape[0]
    groups = width // GW

    barrier = pltpu.get_barrier_semaphore()
    for step in range(1, n):
        pl.semaphore_signal(
            barrier, inc=1, device_id={"chan": lax.rem(me + step, n)}, device_id_type=MESH
        )

    tap_copies = []
    for g in range(groups):
        for p in range(PHASES):
            copy = pltpu.make_async_copy(
                position_weight.at[pl.ds(g * GW, GW), pl.ds(p * SPAN * GW, SPAN * GW)],
                taps.at[g, pl.ds(p * GW, GW), :],
                taps_sem.at[g, p],
            )
            copy.start()
            tap_copies.append(copy)

    pl.semaphore_wait(barrier, n - 1)

    def block(index):
        return gathered.at[pl.ds(pl.multiple_of(index * rows, 16), rows), :]

    chip_copies = []
    for step in range(1, chips):
        copy = pltpu.make_async_remote_copy(
            src_ref=normed,
            dst_ref=block(me),
            send_sem=send_sem.at[step],
            recv_sem=recv_sem.at[step],
            device_id={"chan": lax.rem(chip + step, chips) * 2 + core},
            device_id_type=MESH,
        )
        copy.start()
        chip_copies.append(copy)
    first_pair = pltpu.make_async_remote_copy(
        src_ref=normed,
        dst_ref=block(me),
        send_sem=pair_send.at[0],
        recv_sem=pair_recv.at[0],
        device_id={"chan": pair},
        device_id_type=MESH,
    )
    first_pair.start()

    def project(index, source):
        values = jnp.dot(source[...], project_weight[...], preferred_element_type=jnp.float32)
        values = (values + params[0:1, :]).astype(jnp.bfloat16).astype(jnp.float32)
        frame = (
            shard * frames
            - HALF
            + index * rows
            + lax.broadcasted_iota(jnp.int32, (rows, 1), 0)
        )
        inside = (frame >= 0) & (frame < shards * frames)
        x32[pl.ds(pl.multiple_of(index * rows, 8), rows), :] = jnp.where(inside, values, 0.0)

    x32[n * rows :, :] = jnp.zeros_like(x32[n * rows :, :])
    x2[...] = jnp.zeros_like(x2)
    project(me, normed)
    first_pair.wait_recv()
    project(pair, block(pair))
    forwards = []
    for step in range(1, chips):
        other = lax.rem(chip + chips - step, chips) * 2 + core
        chip_copies[step - 1].wait_recv()
        copy = pltpu.make_async_remote_copy(
            src_ref=block(other),
            dst_ref=block(other),
            send_sem=pair_send.at[step],
            recv_sem=pair_recv.at[step],
            device_id={"chan": pair},
            device_id_type=MESH,
        )
        copy.start()
        forwards.append(copy)
        project(other, block(other))
    for step in range(1, chips):
        other = lax.rem(chip + chips - step, chips) * 2 + 1 - core
        forwards[step - 1].wait_recv()
        project(other, block(other))

    length = frames + K
    chunk = length // 4
    for g in range(groups):
        lanes = slice(g * GW, (g + 1) * GW)
        x2[0:length, :] = jnp.concatenate(
            [x32[0:length, lanes], x32[1 : length + 1, lanes]], axis=1
        )
        for q in range(SPAN // 4):
            window[:, q * 2 * GW : (q + 1) * 2 * GW] = x2[
                2 * q : 2 * q + length + 16, :
            ].astype(jnp.bfloat16)
        for p in range(PHASES):
            tap_copies[g * PHASES + p].wait()
        middle = SPAN // 2 * GW

        @pl.loop(0, 4)
        def _(m):
            start = pl.multiple_of(m * chunk, 16)
            partial[pl.ds(start, chunk), :] = lax.dot_general(
                window[pl.ds(start, chunk), :],
                taps[g, :, 0:middle],
                NT,
                preferred_element_type=jnp.float32,
            ) + lax.dot_general(
                window[pl.ds(pl.multiple_of(start + 16, 16), chunk), :],
                taps[g, :, middle : 2 * middle],
                NT,
                preferred_element_type=jnp.float32,
            )

        total = partial[0:frames, 0:GW]
        for p in range(1, PHASES):
            total = total + partial[p * SPAN : p * SPAN + frames, p * GW : (p + 1) * GW]
        positional[:, lanes] = total

    tile = 128

    @pl.loop(0, frames // tile)
    def _(m):
        start = pl.multiple_of(m * tile, tile)
        values = x32[pl.ds(start + HALF, tile), :] + gelu_exact(
            positional[pl.ds(start, tile), :] + params[1:2, :]
        )
        turned = values.T
        summed[:, pl.ds(start, tile)] = turned
        stats[me, 0:1, pl.ds(start, tile)] = jnp.sum(turned, axis=0, keepdims=True)
        stats[me, 1:2, pl.ds(start, tile)] = jnp.sum(turned * turned, axis=0, keepdims=True)

    stat_copies = []
    for step in range(1, n):
        copy = pltpu.make_async_remote_copy(
            src_ref=stats.at[me],
            dst_ref=stats.at[me],
            send_sem=stat_send.at[step],
            recv_sem=stat_recv.at[step],
            device_id={"chan": lax.rem(me + step, n)},
            device_id_type=MESH,
        )
        copy.start()
        stat_copies.append(copy)
    gain_bias = params[...].T
    for copy in stat_copies:
        copy.wait_recv()
    gain, bias = gain_bias[:, 2:3], gain_bias[:, 3:4]

    @pl.loop(0, frames // tile)
    def _(m):
        start = pl.multiple_of(m * tile, tile)
        both = stats[0, 0:2, pl.ds(start, tile)]
        for index in range(1, n):
            both = both + stats[index, 0:2, pl.ds(start, tile)]
        mean = both[0:1] / model_width
        scale = lax.rsqrt(both[1:2] / model_width - mean * mean + 1e-05)
        out[:, pl.ds(start, tile)] = (
            (summed[:, pl.ds(start, tile)] - mean) * scale * gain + bias
        ).astype(jnp.bfloat16)

    for copy in chip_copies + [first_pair] + forwards + stat_copies:
        copy.wait_send()


def tail(normed, project_weight, params, position_weight, n, frames, model_width):
    rows, channels = normed.shape
    width = project_weight.shape[1]
    groups = width // GW
    length = frames + K
    vmem = pl.BlockSpec(memory_space=pltpu.VMEM)
    dma = pltpu.SemaphoreType.DMA
    return pl.pallas_call(
        functools.partial(tail_kernel, n, frames, rows, model_width),
        out_shape=jax.ShapeDtypeStruct((width, frames), jnp.bfloat16),
        in_specs=[vmem, vmem, vmem, pl.BlockSpec(memory_space=pl.ANY)],
        out_specs=vmem,
        scratch_shapes=[
            pltpu.VMEM((n * rows, channels), jnp.bfloat16),
            pltpu.VMEM((groups, PHASES * GW, SPAN * GW), jnp.bfloat16),
            pltpu.VMEM((n * rows + 64, width), jnp.float32),
            pltpu.VMEM((length + 64, 2 * GW), jnp.float32),
            pltpu.VMEM((length + 16, SPAN // 2 * GW), jnp.bfloat16),
            pltpu.VMEM((length, PHASES * GW), jnp.float32),
            pltpu.VMEM((frames, width), jnp.float32),
            pltpu.VMEM((width, frames), jnp.float32),
            pltpu.VMEM((n, 2, frames), jnp.float32),
            dma((groups, PHASES)),
            dma((n // 2,)),
            dma((n // 2,)),
            dma((n // 2,)),
            dma((n // 2,)),
            dma((n,)),
            dma((n,)),
        ],
        compiler_params=pltpu.CompilerParams(
            collective_id=0, has_side_effects=True, vmem_limit_bytes=48 * 1024 * 1024
        ),
        name="tail",
    )(normed, project_weight, params, position_weight)


def feature_norm(rows, gain, bias):
    values = rows.astype(jnp.float32)
    mean = jnp.mean(values, axis=1, keepdims=True)
    centred = values - mean
    spread = jnp.mean(centred * centred, axis=1, keepdims=True)
    return (centred * lax.rsqrt(spread + 1e-05) * gain + bias).astype(jnp.bfloat16)


def local(
    waveform,
    first_weight,
    instance_gain,
    instance_bias,
    second_weight,
    third_weight,
    feature_gain,
    feature_bias,
    project_weight,
    project_bias,
    position_weight,
    position_bias,
    final_gain,
    final_bias,
):
    n = lax.axis_size("chan")
    me = lax.axis_index("chan")
    shards = lax.axis_size("tm")
    shard = lax.axis_index("tm")
    frames = waveform.shape[0] // 20
    rows = rows_per_device(frames, n)
    channels = feature_gain.shape[0]
    width = project_weight.shape[1]
    model_width = width * n

    weights = lax.all_gather(
        jnp.concatenate([second_weight, third_weight], 0), "chan", axis=2, tiled=True
    )
    second_full = weights[:3].reshape(3 * channels, channels)
    third_full = weights[3:].reshape(3 * channels, channels)
    small = lax.all_gather(
        jnp.concatenate(
            [first_weight.astype(jnp.float32), instance_gain[None], instance_bias[None]], 0
        ),
        "chan",
        axis=1,
        tiled=True,
    )
    first_full = small[:10].astype(jnp.bfloat16)
    gain, offset = small[10], small[11]

    after = 20 * (n * rows - HALF - frames) + 40
    before = 20 * HALF
    samples = jnp.concatenate(
        [shifted(waveform[-before:], "tm", 1), waveform, shifted(waveform[:after], "tm", -1)]
    )
    mine = lax.dynamic_slice_in_dim(samples, me * rows * 20, (rows + 2) * 20)
    mine = mine.reshape(rows + 2, 20)
    patches = jnp.concatenate([mine[:-1], mine[1:, :5]], axis=1)
    band = jnp.concatenate(
        [jnp.pad(first_full, ((5 * f, 15 - 5 * f), (0, 0))) for f in range(4)], axis=1
    )
    conv = jnp.dot(patches, band, preferred_element_type=jnp.float32)
    place = me * rows - HALF + jnp.arange(rows + 1)[:, None]
    counted = (place >= 0) & (place < frames) & (jnp.arange(rows + 1)[:, None] < rows)
    kept = jnp.where(counted, conv, 0.0)
    sums = jnp.stack([jnp.sum(kept, axis=0), jnp.sum(kept * kept, axis=0)])
    sums = jnp.sum(sums.reshape(2, 4, channels), axis=1)
    sums = lax.psum(sums, ("tm", "chan"))
    count = 4 * frames * shards
    mean_first = sums[0] / count
    var_first = sums[1] / count - mean_first * mean_first
    scale = lax.rsqrt(var_first + 1e-05)
    spread = [jnp.tile(v, 4) for v in (mean_first, scale, gain, offset)]
    first = gelu_exact((conv - spread[0]) * spread[1] * spread[2] + spread[3])
    inside = (shard * frames + place >= 0) & (shard * frames + place < shards * frames)
    first = jnp.where(inside, first, 0.0).astype(jnp.bfloat16)

    def dot(a, b):
        return jnp.dot(a, b, preferred_element_type=jnp.float32)

    c = channels
    second_even = gelu_exact(dot(first[:, : 3 * c], second_full)).astype(jnp.bfloat16)
    second_odd = gelu_exact(
        dot(first[:-1, 2 * c :], second_full[: 2 * c]) + dot(first[1:, :c], second_full[2 * c :])
    ).astype(jnp.bfloat16)
    third = gelu_exact(
        dot(second_even[:-1], third_full[:c])
        + dot(second_odd, third_full[c : 2 * c])
        + dot(second_even[1:], third_full[2 * c :])
    ).astype(jnp.bfloat16)
    normed = feature_norm(third, feature_gain, feature_bias)

    bias_here = lax.dynamic_slice_in_dim(project_bias, me * width, width)
    params = jnp.stack([bias_here, position_bias, final_gain, final_bias])
    params = jnp.pad(params, ((0, 4), (0, 0)))
    return tail(normed, project_weight, params, position_weight, n, frames, model_width)


def solution(mesh):
    return jax.shard_map(
        local,
        mesh=mesh,
        in_specs=(
            P(("rec", "tm")),
            P(None, "chan"),
            P("chan"),
            P("chan"),
            P(None, None, "chan"),
            P(None, None, "chan"),
            P(),
            P(),
            P(None, "chan"),
            P(),
            P("chan", None),
            P("chan"),
            P("chan"),
            P("chan"),
        ),
        out_specs=P("chan", ("rec", "tm")),
        check_vma=False,
    )
```

```python
import functools

import jax
import jax.numpy as jnp
from jax import lax
from jax.experimental import pallas as pl
from jax.experimental.pallas import tpu as pltpu
from jax.sharding import PartitionSpec as P

K = 128
GW = 64
HALF = K // 2
SPAN = 32
PHASES = K // SPAN
MESH = pl.DeviceIdType.MESH
NT = (((1,), (1,)), ((), ()))


def gelu_exact(values):
    return 0.5 * values * (1.0 + lax.erf(values * 0.7071067811865476))


def rows_per_device(frames, count):
    return -(-(frames + K) // (16 * count)) * 16


def encoder_kernel(
    n,
    shards,
    frames,
    rows,
    model_width,
    waveform,
    small,
    second_weight,
    third_weight,
    feature,
    project_weight,
    params,
    position_weight,
    out,
    samples,
    sample32,
    smalls,
    band32,
    conv,
    first,
    shift32,
    second,
    slots,
    full,
    own_stats,
    chan_stats,
    tm_stats,
    normed,
    gathered,
    taps,
    x32,
    x2,
    window,
    partial,
    positional,
    summed,
    stats,
    own_sem,
    halo_send,
    halo_recv,
    small_send,
    small_recv,
    weight_send,
    weight_recv,
    weight_pair_send,
    weight_pair_recv,
    moment_send,
    moment_recv,
    total_send,
    total_recv,
    taps_sem,
    send_sem,
    recv_sem,
    pair_send,
    pair_recv,
    stat_send,
    stat_recv,
):
    me = lax.axis_index("chan")
    shard = lax.axis_index("tm")
    chips = n // 2
    chip, core = me // 2, lax.rem(me, 2)
    pair = chip * 2 + 1 - core
    width = out.shape[0]
    groups = width // GW
    channels = feature.shape[1]
    part = channels // n
    after = samples.shape[0] - HALF - frames
    sent = []

    def send(source, target, send_at, recv_at, **device):
        copy = pltpu.make_async_remote_copy(
            src_ref=source,
            dst_ref=target,
            send_sem=send_at,
            recv_sem=recv_at,
            device_id=device,
            device_id_type=MESH,
        )
        copy.start()
        sent.append(copy)
        return copy

    own_copies = []
    for index, weight in enumerate((second_weight, third_weight)):
        copy = pltpu.make_async_copy(weight, slots.at[index, me], own_sem.at[index])
        copy.start()
        own_copies.append(copy)

    barrier = pltpu.get_barrier_semaphore()
    for step in range(1, n):
        pl.semaphore_signal(
            barrier, inc=1, device_id={"chan": lax.rem(me + step, n)}, device_id_type=MESH
        )
    for step in range(1, shards):
        pl.semaphore_signal(
            barrier, inc=1, device_id={"tm": lax.rem(shard + step, shards)}, device_id_type=MESH
        )
    pl.semaphore_wait(barrier, n + shards - 2)

    following = send(
        waveform.at[pl.ds(0, after), :],
        samples.at[pl.ds(HALF + frames, after), :],
        halo_send.at[0],
        halo_recv.at[0],
        tm=lax.rem(shard + shards - 1, shards),
    )
    leading = send(
        waveform.at[pl.ds(frames - HALF, HALF), :],
        samples.at[pl.ds(0, HALF), :],
        halo_send.at[1],
        halo_recv.at[1],
        tm=lax.rem(shard + 1, shards),
    )
    small_copies = [
        send(
            small,
            smalls.at[me],
            small_send.at[step],
            small_recv.at[step],
            chan=lax.rem(me + step, n),
        )
        for step in range(1, n)
    ]
    weight_chip, weight_pair = [], []
    for index, weight in enumerate((second_weight, third_weight)):
        weight_chip.append(
            [
                send(
                    weight,
                    slots.at[index, me],
                    weight_send.at[index, step],
                    weight_recv.at[index, step],
                    chan=lax.rem(chip + step, chips) * 2 + core,
                )
                for step in range(1, chips)
            ]
        )
        weight_pair.append(
            [
                send(
                    weight,
                    slots.at[index, me],
                    weight_pair_send.at[index, 0],
                    weight_pair_recv.at[index, 0],
                    chan=pair,
                )
            ]
        )

    def forward_weight(index):
        for step in range(1, chips):
            other = lax.rem(chip + chips - step, chips) * 2 + core
            weight_chip[index][step - 1].wait_recv()
            weight_pair[index].append(
                send(
                    slots.at[index, other],
                    slots.at[index, other],
                    weight_pair_send.at[index, step],
                    weight_pair_recv.at[index, step],
                    chan=pair,
                )
            )

    def assemble_weight(index):
        own_copies[index].wait()
        for copy in weight_pair[index]:
            copy.wait_recv()
        for source in range(n):
            full[index, :, source * part : (source + 1) * part] = slots[index, source]

    tap_copies = []
    for g in range(groups):
        for p in range(PHASES):
            copy = pltpu.make_async_copy(
                position_weight.at[pl.ds(g * GW, GW), pl.ds(p * SPAN * GW, SPAN * GW)],
                taps.at[g, pl.ds(p * GW, GW), :],
                taps_sem.at[g, p],
            )
            copy.start()
            tap_copies.append(copy)

    samples[HALF : HALF + frames, :] = waveform[...]
    smalls[me] = small[...]
    following.wait_recv()
    leading.wait_recv()
    for copy in small_copies:
        copy.wait_recv()

    extra = rows + 16
    place = me * rows - HALF + lax.broadcasted_iota(jnp.int32, (rows + 32, 1), 0)
    inside = (shard * frames + place >= 0) & (shard * frames + place < shards * frames)
    row = lax.broadcasted_iota(jnp.int32, (extra, 1), 0)
    counted = (place[:extra] >= 0) & (place[:extra] < frames) & (row < rows)
    held = samples[pl.ds(pl.multiple_of(me * rows, 16), rows + 32), :].astype(jnp.float32)
    sample32[...] = jnp.where(inside, held, 0.0)
    patches = (
        sample32[0:extra, :] + pltpu.roll(sample32[1 : extra + 1, :], 20, axis=1)
    ).astype(jnp.bfloat16)

    band32[...] = jnp.zeros_like(band32)
    for f in range(4):
        for source in range(n):
            at = f * channels + source * part
            band32[5 * f : 5 * f + 10, at : at + part] = smalls[source, 0:10, :]
    moments = jnp.zeros((2, channels), jnp.float32)
    for f in range(4):
        lanes = slice(f * channels, (f + 1) * channels)
        values = jnp.dot(
            patches, band32[:, lanes].astype(jnp.bfloat16), preferred_element_type=jnp.float32
        )
        conv[:, lanes] = values
        kept = jnp.where(counted, values, 0.0)
        moments = moments + jnp.concatenate(
            [jnp.sum(kept, axis=0, keepdims=True), jnp.sum(kept * kept, axis=0, keepdims=True)],
            axis=0,
        )
    own_stats[...] = moments
    chan_stats[me] = moments
    moment_copies = [
        send(
            own_stats,
            chan_stats.at[me],
            moment_send.at[step],
            moment_recv.at[step],
            chan=lax.rem(me + step, n),
        )
        for step in range(1, n)
    ]
    gain = jnp.concatenate([smalls[source, 10:11, :] for source in range(n)], axis=1)
    offset = jnp.concatenate([smalls[source, 11:12, :] for source in range(n)], axis=1)
    for copy in moment_copies:
        copy.wait_recv()
    moments = chan_stats[0]
    for index in range(1, n):
        moments = moments + chan_stats[index]
    tm_stats[shard] = moments
    total_copies = [
        send(
            tm_stats.at[shard],
            tm_stats.at[shard],
            total_send.at[step],
            total_recv.at[step],
            tm=lax.rem(shard + step, shards),
        )
        for step in range(1, shards)
    ]
    x32[n * rows :, :] = jnp.zeros_like(x32[n * rows :, :])
    x2[...] = jnp.zeros_like(x2)
    for copy in total_copies:
        copy.wait_recv()
    moments = tm_stats[0]
    for index in range(1, shards):
        moments = moments + tm_stats[index]
    moments = moments / (4 * frames * shards)
    mean = moments[0:1]
    scale = lax.rsqrt(moments[1:2] - mean * mean + 1e-05)

    for f in range(4):
        lanes = slice(f * channels, (f + 1) * channels)
        values = gelu_exact((conv[:, lanes] - mean) * scale * gain + offset)
        values = jnp.where(inside[:extra], values, 0.0).astype(jnp.bfloat16)
        first[:, lanes] = values
        if f == 0:
            shift32[...] = values.astype(jnp.float32)

    def dot(a, b):
        return jnp.dot(a, b, preferred_element_type=jnp.float32)

    c = channels
    forward_weight(0)
    assemble_weight(0)
    second[0:rows, :] = gelu_exact(
        dot(first[0:rows, 2 * c :], full[0, 0 : 2 * c, :])
        + dot(shift32[1 : rows + 1, :].astype(jnp.bfloat16), full[0, 2 * c :, :])
    ).astype(jnp.bfloat16)
    even = gelu_exact(dot(first[:, 0 : 3 * c], full[0])).astype(jnp.bfloat16)
    shift32[...] = even.astype(jnp.float32)
    forward_weight(1)
    assemble_weight(1)
    third = gelu_exact(
        dot(even[0:rows], full[1, 0:c, :])
        + dot(second[0:rows, :], full[1, c : 2 * c, :])
        + dot(shift32[1 : rows + 1, :].astype(jnp.bfloat16), full[1, 2 * c :, :])
    )
    third = third.astype(jnp.bfloat16).astype(jnp.float32)
    centred = third - jnp.mean(third, axis=1, keepdims=True)
    spread = jnp.mean(centred * centred, axis=1, keepdims=True)
    normed[...] = (
        centred * lax.rsqrt(spread + 1e-05) * feature[0:1, :] + feature[1:2, :]
    ).astype(jnp.bfloat16)

    def block(index):
        return gathered.at[pl.ds(pl.multiple_of(index * rows, 16), rows), :]

    chip_copies = []
    for step in range(1, chips):
        copy = pltpu.make_async_remote_copy(
            src_ref=normed,
            dst_ref=block(me),
            send_sem=send_sem.at[step],
            recv_sem=recv_sem.at[step],
            device_id={"chan": lax.rem(chip + step, chips) * 2 + core},
            device_id_type=MESH,
        )
        copy.start()
        chip_copies.append(copy)
    first_pair = pltpu.make_async_remote_copy(
        src_ref=normed,
        dst_ref=block(me),
        send_sem=pair_send.at[0],
        recv_sem=pair_recv.at[0],
        device_id={"chan": pair},
        device_id_type=MESH,
    )
    first_pair.start()

    def project(index, source):
        values = jnp.dot(source[...], project_weight[...], preferred_element_type=jnp.float32)
        values = (values + params[0:1, :]).astype(jnp.bfloat16).astype(jnp.float32)
        frame = (
            shard * frames
            - HALF
            + index * rows
            + lax.broadcasted_iota(jnp.int32, (rows, 1), 0)
        )
        inside = (frame >= 0) & (frame < shards * frames)
        x32[pl.ds(pl.multiple_of(index * rows, 8), rows), :] = jnp.where(inside, values, 0.0)

    project(me, normed)
    first_pair.wait_recv()
    project(pair, block(pair))
    forwards = []
    for step in range(1, chips):
        other = lax.rem(chip + chips - step, chips) * 2 + core
        chip_copies[step - 1].wait_recv()
        copy = pltpu.make_async_remote_copy(
            src_ref=block(other),
            dst_ref=block(other),
            send_sem=pair_send.at[step],
            recv_sem=pair_recv.at[step],
            device_id={"chan": pair},
            device_id_type=MESH,
        )
        copy.start()
        forwards.append(copy)
        project(other, block(other))
    for step in range(1, chips):
        other = lax.rem(chip + chips - step, chips) * 2 + 1 - core
        forwards[step - 1].wait_recv()
        project(other, block(other))

    length = frames + K
    chunk = length // 4
    for g in range(groups):
        lanes = slice(g * GW, (g + 1) * GW)
        x2[0:length, :] = jnp.concatenate(
            [x32[0:length, lanes], x32[1 : length + 1, lanes]], axis=1
        )
        for q in range(SPAN // 4):
            window[:, q * 2 * GW : (q + 1) * 2 * GW] = x2[
                2 * q : 2 * q + length + 16, :
            ].astype(jnp.bfloat16)
        for p in range(PHASES):
            tap_copies[g * PHASES + p].wait()
        middle = SPAN // 2 * GW

        @pl.loop(0, 4)
        def _(m):
            start = pl.multiple_of(m * chunk, 16)
            partial[pl.ds(start, chunk), :] = lax.dot_general(
                window[pl.ds(start, chunk), :],
                taps[g, :, 0:middle],
                NT,
                preferred_element_type=jnp.float32,
            ) + lax.dot_general(
                window[pl.ds(pl.multiple_of(start + 16, 16), chunk), :],
                taps[g, :, middle : 2 * middle],
                NT,
                preferred_element_type=jnp.float32,
            )

        total = partial[0:frames, 0:GW]
        for p in range(1, PHASES):
            total = total + partial[p * SPAN : p * SPAN + frames, p * GW : (p + 1) * GW]
        positional[:, lanes] = total

    tile = 128

    @pl.loop(0, frames // tile)
    def _(m):
        start = pl.multiple_of(m * tile, tile)
        values = x32[pl.ds(start + HALF, tile), :] + gelu_exact(
            positional[pl.ds(start, tile), :] + params[1:2, :]
        )
        turned = values.T
        summed[:, pl.ds(start, tile)] = turned
        stats[me, 0:1, pl.ds(start, tile)] = jnp.sum(turned, axis=0, keepdims=True)
        stats[me, 1:2, pl.ds(start, tile)] = jnp.sum(turned * turned, axis=0, keepdims=True)

    stat_copies = []
    for step in range(1, n):
        copy = pltpu.make_async_remote_copy(
            src_ref=stats.at[me],
            dst_ref=stats.at[me],
            send_sem=stat_send.at[step],
            recv_sem=stat_recv.at[step],
            device_id={"chan": lax.rem(me + step, n)},
            device_id_type=MESH,
        )
        copy.start()
        stat_copies.append(copy)
    gain_bias = params[...].T
    for copy in stat_copies:
        copy.wait_recv()
    last_gain, last_bias = gain_bias[:, 2:3], gain_bias[:, 3:4]

    @pl.loop(0, frames // tile)
    def _(m):
        start = pl.multiple_of(m * tile, tile)
        both = stats[0, 0:2, pl.ds(start, tile)]
        for index in range(1, n):
            both = both + stats[index, 0:2, pl.ds(start, tile)]
        mean = both[0:1] / model_width
        scale = lax.rsqrt(both[1:2] / model_width - mean * mean + 1e-05)
        out[:, pl.ds(start, tile)] = (
            (summed[:, pl.ds(start, tile)] - mean) * scale * last_gain + last_bias
        ).astype(jnp.bfloat16)

    for copy in sent + chip_copies + [first_pair] + forwards + stat_copies:
        copy.wait_send()


def encoder(
    waveform,
    small,
    second_weight,
    third_weight,
    feature,
    project_weight,
    params,
    position_weight,
    n,
    shards,
    model_width,
):
    frames = waveform.shape[0]
    rows = rows_per_device(frames, n)
    after = -(-(n * rows - HALF - frames + 32) // 16) * 16
    channels = feature.shape[1]
    part = channels // n
    width = project_weight.shape[1]
    groups = width // GW
    length = frames + K
    vmem = pl.BlockSpec(memory_space=pltpu.VMEM)
    anywhere = pl.BlockSpec(memory_space=pl.ANY)
    dma = pltpu.SemaphoreType.DMA
    half = jnp.bfloat16
    single = jnp.float32
    return pl.pallas_call(
        functools.partial(encoder_kernel, n, shards, frames, rows, model_width),
        out_shape=jax.ShapeDtypeStruct((width, frames), half),
        in_specs=[vmem, vmem, anywhere, anywhere, vmem, vmem, vmem, anywhere],
        out_specs=vmem,
        scratch_shapes=[
            pltpu.VMEM((HALF + frames + after, 128), half),
            pltpu.VMEM((rows + 32, 128), single),
            pltpu.VMEM((n, 16, part), single),
            pltpu.VMEM((128, 4 * channels), single),
            pltpu.VMEM((rows + 16, 4 * channels), single),
            pltpu.VMEM((rows + 16, 4 * channels), half),
            pltpu.VMEM((rows + 16, channels), single),
            pltpu.VMEM((rows, channels), half),
            pltpu.VMEM((2, n, 3 * channels, part), half),
            pltpu.VMEM((2, 3 * channels, channels), half),
            pltpu.VMEM((2, channels), single),
            pltpu.VMEM((n, 2, channels), single),
            pltpu.VMEM((shards, 2, channels), single),
            pltpu.VMEM((rows, channels), half),
            pltpu.VMEM((n * rows, channels), half),
            pltpu.VMEM((groups, PHASES * GW, SPAN * GW), half),
            pltpu.VMEM((n * rows + 64, width), single),
            pltpu.VMEM((length + 64, 2 * GW), single),
            pltpu.VMEM((length + 16, SPAN // 2 * GW), half),
            pltpu.VMEM((length, PHASES * GW), single),
            pltpu.VMEM((frames, width), single),
            pltpu.VMEM((width, frames), single),
            pltpu.VMEM((n, 2, frames), single),
            dma((2,)),
            dma((2,)),
            dma((2,)),
            dma((n,)),
            dma((n,)),
            dma((2, n // 2)),
            dma((2, n // 2)),
            dma((2, n // 2)),
            dma((2, n // 2)),
            dma((n,)),
            dma((n,)),
            dma((shards,)),
            dma((shards,)),
            dma((groups, PHASES)),
            dma((n // 2,)),
            dma((n // 2,)),
            dma((n // 2,)),
            dma((n // 2,)),
            dma((n,)),
            dma((n,)),
        ],
        compiler_params=pltpu.CompilerParams(
            collective_id=0, has_side_effects=True, vmem_limit_bytes=56 * 1024 * 1024
        ),
        name="encoder",
    )(
        waveform,
        small,
        second_weight,
        third_weight,
        feature,
        project_weight,
        params,
        position_weight,
    )


def local(
    waveform,
    first_weight,
    instance_gain,
    instance_bias,
    second_weight,
    third_weight,
    feature_gain,
    feature_bias,
    project_weight,
    project_bias,
    position_weight,
    position_bias,
    final_gain,
    final_bias,
):
    n = lax.axis_size("chan")
    me = lax.axis_index("chan")
    shards = lax.axis_size("tm")
    channels, part = second_weight.shape[1:]
    width = project_weight.shape[1]
    blocks = jnp.pad(waveform.reshape(-1, 20), ((0, 0), (0, 108)))
    small = jnp.concatenate(
        [
            first_weight.astype(jnp.float32),
            instance_gain[None],
            instance_bias[None],
            jnp.zeros((4, part), jnp.float32),
        ],
        0,
    )
    bias_here = lax.dynamic_slice_in_dim(project_bias, me * width, width)
    params = jnp.stack([bias_here, position_bias, final_gain, final_bias])
    params = jnp.pad(params, ((0, 4), (0, 0)))
    feature = jnp.stack([feature_gain, feature_bias])
    return encoder(
        blocks,
        small,
        second_weight.reshape(3 * channels, part),
        third_weight.reshape(3 * channels, part),
        feature,
        project_weight,
        params,
        position_weight,
        n,
        shards,
        width * n,
    )


def solution(mesh):
    return jax.shard_map(
        local,
        mesh=mesh,
        in_specs=(
            P(("rec", "tm")),
            P(None, "chan"),
            P("chan"),
            P("chan"),
            P(None, None, "chan"),
            P(None, None, "chan"),
            P(),
            P(),
            P(None, "chan"),
            P(),
            P("chan", None),
            P("chan"),
            P("chan"),
            P("chan"),
        ),
        out_specs=P("chan", ("rec", "tm")),
        check_vma=False,
    )
```

```python
import functools

import jax
import jax.numpy as jnp
from jax import lax
from jax.experimental import pallas as pl
from jax.experimental.pallas import tpu as pltpu
from jax.sharding import PartitionSpec as P

K = 128
GW = 64
HALF = K // 2
SPAN = 32
PHASES = K // SPAN
MESH = pl.DeviceIdType.MESH
NT = (((1,), (1,)), ((), ()))


def gelu_exact(values):
    return 0.5 * values * (1.0 + lax.erf(values * 0.7071067811865476))


def rows_per_device(frames, count):
    return -(-(frames + K) // (16 * count)) * 16


def encoder_kernel(
    n,
    shards,
    frames,
    rows,
    model_width,
    wave,
    first_weight,
    instance_gain,
    instance_bias,
    second_weight,
    third_weight,
    feature_gain,
    feature_bias,
    project_weight,
    project_bias,
    position_weight,
    position_bias,
    summed,
    norm,
    waveform,
    params,
    samples,
    sample32,
    smalls,
    band32,
    conv,
    first,
    shift32,
    second,
    slots,
    full,
    own_stats,
    chan_stats,
    tm_stats,
    normed,
    gathered,
    taps,
    x32,
    x2,
    window,
    partial,
    positional,
    stats,
    own_sem,
    halo_send,
    halo_recv,
    small_send,
    small_recv,
    weight_send,
    weight_recv,
    weight_pair_send,
    weight_pair_recv,
    rec_send,
    rec_recv,
    moment_send,
    moment_recv,
    total_send,
    total_recv,
    taps_sem,
    send_sem,
    recv_sem,
    pair_send,
    pair_recv,
    stat_send,
    stat_recv,
):
    me = lax.axis_index("chan")
    shard = lax.axis_index("tm")
    rec = lax.axis_index("rec")
    recs = lax.axis_size("rec")
    chips = n // 2
    chip, core = me // 2, lax.rem(me, 2)
    pair = chip * 2 + 1 - core
    width = summed.shape[0]
    groups = width // GW
    channels = feature_gain.shape[1]
    part = channels // n
    after = samples.shape[0] - HALF - frames
    sent = []

    def send(source, target, send_at, recv_at, **device):
        copy = pltpu.make_async_remote_copy(
            src_ref=source,
            dst_ref=target,
            send_sem=send_at,
            recv_sem=recv_at,
            device_id=device,
            device_id_type=MESH,
        )
        copy.start()
        sent.append(copy)
        return copy

    own_copies = []
    for index, weight in enumerate((second_weight, third_weight)):
        copy = pltpu.make_async_copy(weight, slots.at[index, me], own_sem.at[index])
        copy.start()
        own_copies.append(copy)

    barrier = pltpu.get_barrier_semaphore()
    for step in range(1, n):
        pl.semaphore_signal(
            barrier, inc=1, device_id={"chan": lax.rem(me + step, n)}, device_id_type=MESH
        )
    for step in range(1, shards):
        pl.semaphore_signal(
            barrier, inc=1, device_id={"tm": lax.rem(shard + step, shards)}, device_id_type=MESH
        )
    for step in range(1, recs):
        pl.semaphore_signal(
            barrier, inc=1, device_id={"rec": lax.rem(rec + step, recs)}, device_id_type=MESH
        )
    waveform[...] = jnp.zeros_like(waveform)
    waveform[:, 0:20] = wave[...]
    smalls[me] = jnp.concatenate(
        [
            first_weight[...].astype(jnp.float32),
            instance_gain[...],
            instance_bias[...],
            jnp.zeros((4, part), jnp.float32),
        ],
        axis=0,
    )
    pl.semaphore_wait(barrier, n + shards + recs - 3)

    following = send(
        waveform.at[pl.ds(0, after), :],
        samples.at[pl.ds(HALF + frames, after), :],
        halo_send.at[0],
        halo_recv.at[0],
        tm=lax.rem(shard + shards - 1, shards),
    )
    leading = send(
        waveform.at[pl.ds(frames - HALF, HALF), :],
        samples.at[pl.ds(0, HALF), :],
        halo_send.at[1],
        halo_recv.at[1],
        tm=lax.rem(shard + 1, shards),
    )
    small_copies = [
        send(
            smalls.at[me],
            smalls.at[me],
            small_send.at[step],
            small_recv.at[step],
            chan=lax.rem(me + step, n),
        )
        for step in range(1, n)
    ]
    weight_chip, weight_pair, weight_rec = [], [], [[], []]
    depth = 3 * channels // recs

    def share(owner):
        return pl.ds(pl.multiple_of(owner * depth, 16), depth)

    for index, weight in enumerate((second_weight, third_weight)):
        weight_chip.append(
            [
                send(
                    weight.at[share(rec), :],
                    slots.at[index, me, share(rec), :],
                    weight_send.at[index, step],
                    weight_recv.at[index, step],
                    chan=lax.rem(chip + step, chips) * 2 + core,
                )
                for step in range(1, chips)
            ]
        )
        weight_pair.append(
            [
                send(
                    weight,
                    slots.at[index, me],
                    weight_pair_send.at[index, 0, 0],
                    weight_pair_recv.at[index, 0, 0],
                    chan=pair,
                )
            ]
        )

    def forward_chip(index):
        for step in range(1, chips):
            other = lax.rem(chip + chips - step, chips) * 2 + core
            piece = slots.at[index, other, share(rec), :]
            weight_chip[index][step - 1].wait_recv()
            for turn in range(1, recs):
                weight_rec[index].append(
                    send(
                        piece,
                        piece,
                        rec_send.at[index, step, turn],
                        rec_recv.at[index, step, turn],
                        rec=lax.rem(rec + turn, recs),
                    )
                )
            weight_pair[index].append(
                send(
                    piece,
                    piece,
                    weight_pair_send.at[index, step, 0],
                    weight_pair_recv.at[index, step, 0],
                    chan=pair,
                )
            )

    def forward_rec(index):
        arrivals = iter(weight_rec[index])
        for step in range(1, chips):
            other = lax.rem(chip + chips - step, chips) * 2 + core
            for turn in range(1, recs):
                piece = slots.at[index, other, share(lax.rem(rec + recs - turn, recs)), :]
                next(arrivals).wait_recv()
                weight_pair[index].append(
                    send(
                        piece,
                        piece,
                        weight_pair_send.at[index, step, turn],
                        weight_pair_recv.at[index, step, turn],
                        chan=pair,
                    )
                )

    def assemble_weight(index):
        own_copies[index].wait()
        for copy in weight_pair[index]:
            copy.wait_recv()
        for source in range(n):
            full[index, :, source * part : (source + 1) * part] = slots[index, source]

    tap_copies = []
    for g in range(groups):
        for p in range(PHASES):
            copy = pltpu.make_async_copy(
                position_weight.at[pl.ds(g * GW, GW), pl.ds(p * SPAN * GW, SPAN * GW)],
                taps.at[g, pl.ds(p * GW, GW), :],
                taps_sem.at[g, p],
            )
            copy.start()
            tap_copies.append(copy)

    samples[HALF : HALF + frames, :] = waveform[...]
    chosen = project_bias[:, 0:width]
    for source in range(1, n):
        chosen = jnp.where(me == source, project_bias[:, source * width : (source + 1) * width], chosen)
    params[...] = jnp.concatenate(
        [chosen, position_bias[...], jnp.zeros((6, width), jnp.float32)], axis=0
    )
    following.wait_recv()
    leading.wait_recv()
    for copy in small_copies:
        copy.wait_recv()

    extra = rows + 16
    place = me * rows - HALF + lax.broadcasted_iota(jnp.int32, (rows + 32, 1), 0)
    inside = (shard * frames + place >= 0) & (shard * frames + place < shards * frames)
    row = lax.broadcasted_iota(jnp.int32, (extra, 1), 0)
    counted = (place[:extra] >= 0) & (place[:extra] < frames) & (row < rows)
    held = samples[pl.ds(pl.multiple_of(me * rows, 16), rows + 32), :].astype(jnp.float32)
    sample32[...] = jnp.where(inside, held, 0.0)
    patches = (
        sample32[0:extra, :] + pltpu.roll(sample32[1 : extra + 1, :], 20, axis=1)
    ).astype(jnp.bfloat16)

    band32[...] = jnp.zeros_like(band32)
    for f in range(4):
        for source in range(n):
            at = f * channels + source * part
            band32[5 * f : 5 * f + 10, at : at + part] = smalls[source, 0:10, :]
    moments = jnp.zeros((2, channels), jnp.float32)
    for f in range(4):
        lanes = slice(f * channels, (f + 1) * channels)
        values = jnp.dot(
            patches, band32[:, lanes].astype(jnp.bfloat16), preferred_element_type=jnp.float32
        )
        conv[:, lanes] = values
        kept = jnp.where(counted, values, 0.0)
        moments = moments + jnp.concatenate(
            [jnp.sum(kept, axis=0, keepdims=True), jnp.sum(kept * kept, axis=0, keepdims=True)],
            axis=0,
        )
    own_stats[...] = moments
    chan_stats[me] = moments
    moment_copies = [
        send(
            own_stats,
            chan_stats.at[me],
            moment_send.at[step],
            moment_recv.at[step],
            chan=lax.rem(me + step, n),
        )
        for step in range(1, n)
    ]
    gain = jnp.concatenate([smalls[source, 10:11, :] for source in range(n)], axis=1)
    offset = jnp.concatenate([smalls[source, 11:12, :] for source in range(n)], axis=1)
    forward_chip(0)
    for copy in moment_copies:
        copy.wait_recv()
    moments = chan_stats[0]
    for index in range(1, n):
        moments = moments + chan_stats[index]
    tm_stats[shard] = moments
    total_copies = [
        send(
            tm_stats.at[shard],
            tm_stats.at[shard],
            total_send.at[step],
            total_recv.at[step],
            tm=lax.rem(shard + step, shards),
        )
        for step in range(1, shards)
    ]
    x32[n * rows :, :] = jnp.zeros_like(x32[n * rows :, :])
    x2[...] = jnp.zeros_like(x2)
    for copy in total_copies:
        copy.wait_recv()
    moments = tm_stats[0]
    for index in range(1, shards):
        moments = moments + tm_stats[index]
    moments = moments / (4 * frames * shards)
    mean = moments[0:1]
    scale = lax.rsqrt(moments[1:2] - mean * mean + 1e-05)

    forward_chip(1)
    forward_rec(0)
    for f in range(4):
        lanes = slice(f * channels, (f + 1) * channels)
        values = gelu_exact((conv[:, lanes] - mean) * scale * gain + offset)
        values = jnp.where(inside[:extra], values, 0.0).astype(jnp.bfloat16)
        first[:, lanes] = values
        if f == 0:
            shift32[...] = values.astype(jnp.float32)

    def dot(a, b):
        return jnp.dot(a, b, preferred_element_type=jnp.float32)

    c = channels
    forward_rec(1)
    assemble_weight(0)
    second[0:rows, :] = gelu_exact(
        dot(first[0:rows, 2 * c :], full[0, 0 : 2 * c, :])
        + dot(shift32[1 : rows + 1, :].astype(jnp.bfloat16), full[0, 2 * c :, :])
    ).astype(jnp.bfloat16)
    even = gelu_exact(dot(first[:, 0 : 3 * c], full[0])).astype(jnp.bfloat16)
    shift32[...] = even.astype(jnp.float32)
    assemble_weight(1)
    third = gelu_exact(
        dot(even[0:rows], full[1, 0:c, :])
        + dot(second[0:rows, :], full[1, c : 2 * c, :])
        + dot(shift32[1 : rows + 1, :].astype(jnp.bfloat16), full[1, 2 * c :, :])
    )
    third = third.astype(jnp.bfloat16).astype(jnp.float32)
    centred = third - jnp.mean(third, axis=1, keepdims=True)
    spread = jnp.mean(centred * centred, axis=1, keepdims=True)
    normed[...] = (
        centred * lax.rsqrt(spread + 1e-05) * feature_gain[...] + feature_bias[...]
    ).astype(jnp.bfloat16)

    def block(index):
        return gathered.at[pl.ds(pl.multiple_of(index * rows, 16), rows), :]

    chip_copies = []
    for step in range(1, chips):
        copy = pltpu.make_async_remote_copy(
            src_ref=normed,
            dst_ref=block(me),
            send_sem=send_sem.at[step],
            recv_sem=recv_sem.at[step],
            device_id={"chan": lax.rem(chip + step, chips) * 2 + core},
            device_id_type=MESH,
        )
        copy.start()
        chip_copies.append(copy)
    first_pair = pltpu.make_async_remote_copy(
        src_ref=normed,
        dst_ref=block(me),
        send_sem=pair_send.at[0],
        recv_sem=pair_recv.at[0],
        device_id={"chan": pair},
        device_id_type=MESH,
    )
    first_pair.start()

    def project(index, source):
        values = jnp.dot(source[...], project_weight[...], preferred_element_type=jnp.float32)
        values = (values + params[0:1, :]).astype(jnp.bfloat16).astype(jnp.float32)
        frame = (
            shard * frames
            - HALF
            + index * rows
            + lax.broadcasted_iota(jnp.int32, (rows, 1), 0)
        )
        inside = (frame >= 0) & (frame < shards * frames)
        x32[pl.ds(pl.multiple_of(index * rows, 8), rows), :] = jnp.where(inside, values, 0.0)

    project(me, normed)
    first_pair.wait_recv()
    project(pair, block(pair))
    forwards = []
    for step in range(1, chips):
        other = lax.rem(chip + chips - step, chips) * 2 + core
        chip_copies[step - 1].wait_recv()
        copy = pltpu.make_async_remote_copy(
            src_ref=block(other),
            dst_ref=block(other),
            send_sem=pair_send.at[step],
            recv_sem=pair_recv.at[step],
            device_id={"chan": pair},
            device_id_type=MESH,
        )
        copy.start()
        forwards.append(copy)
        project(other, block(other))
    for step in range(1, chips):
        other = lax.rem(chip + chips - step, chips) * 2 + 1 - core
        forwards[step - 1].wait_recv()
        project(other, block(other))

    length = frames + K
    chunk = length // 4
    for g in range(groups):
        lanes = slice(g * GW, (g + 1) * GW)
        x2[0:length, :] = jnp.concatenate(
            [x32[0:length, lanes], x32[1 : length + 1, lanes]], axis=1
        )
        for q in range(SPAN // 4):
            window[:, q * 2 * GW : (q + 1) * 2 * GW] = x2[
                2 * q : 2 * q + length + 16, :
            ].astype(jnp.bfloat16)
        for p in range(PHASES):
            tap_copies[g * PHASES + p].wait()
        middle = SPAN // 2 * GW

        @pl.loop(0, 4)
        def _(m):
            start = pl.multiple_of(m * chunk, 16)
            partial[pl.ds(start, chunk), :] = lax.dot_general(
                window[pl.ds(start, chunk), :],
                taps[g, :, 0:middle],
                NT,
                preferred_element_type=jnp.float32,
            ) + lax.dot_general(
                window[pl.ds(pl.multiple_of(start + 16, 16), chunk), :],
                taps[g, :, middle : 2 * middle],
                NT,
                preferred_element_type=jnp.float32,
            )

        total = partial[0:frames, 0:GW]
        for p in range(1, PHASES):
            total = total + partial[p * SPAN : p * SPAN + frames, p * GW : (p + 1) * GW]
        positional[:, lanes] = total

    tile = 128

    @pl.loop(0, frames // tile)
    def _(m):
        start = pl.multiple_of(m * tile, tile)
        values = x32[pl.ds(start + HALF, tile), :] + gelu_exact(
            positional[pl.ds(start, tile), :] + params[1:2, :]
        )
        turned = values.T
        summed[:, pl.ds(start, tile)] = turned
        stats[me, 0:1, pl.ds(start, tile)] = jnp.sum(turned, axis=0, keepdims=True)
        stats[me, 1:2, pl.ds(start, tile)] = jnp.sum(turned * turned, axis=0, keepdims=True)

    stat_copies = []
    for step in range(1, n):
        copy = pltpu.make_async_remote_copy(
            src_ref=stats.at[me],
            dst_ref=stats.at[me],
            send_sem=stat_send.at[step],
            recv_sem=stat_recv.at[step],
            device_id={"chan": lax.rem(me + step, n)},
            device_id_type=MESH,
        )
        copy.start()
        stat_copies.append(copy)
    for copy in stat_copies:
        copy.wait_recv()
    both = stats[0]
    for index in range(1, n):
        both = both + stats[index]
    mean = both[0:1] / model_width
    norm[0:1, :] = mean
    norm[1:2, :] = lax.rsqrt(both[1:2] / model_width - mean * mean + 1e-05)

    for copy in sent + chip_copies + [first_pair] + forwards + stat_copies:
        copy.wait_send()


def encoder(
    waveform,
    first_weight,
    instance_gain,
    instance_bias,
    second_weight,
    third_weight,
    feature_gain,
    feature_bias,
    project_weight,
    project_bias,
    position_weight,
    position_bias,
    n,
    shards,
    model_width,
):
    frames = waveform.shape[0]
    rows = rows_per_device(frames, n)
    after = -(-(n * rows - HALF - frames + 32) // 16) * 16
    channels = feature_gain.shape[1]
    part = channels // n
    recs = lax.axis_size("rec")
    width = project_weight.shape[1]
    groups = width // GW
    length = frames + K
    vmem = pl.BlockSpec(memory_space=pltpu.VMEM)
    anywhere = pl.BlockSpec(memory_space=pl.ANY)
    dma = pltpu.SemaphoreType.DMA
    half = jnp.bfloat16
    single = jnp.float32
    return pl.pallas_call(
        functools.partial(encoder_kernel, n, shards, frames, rows, model_width),
        out_shape=[
            jax.ShapeDtypeStruct((width, frames), single),
            jax.ShapeDtypeStruct((2, frames), single),
        ],
        in_specs=[vmem] * 4 + [anywhere] * 2 + [vmem] * 4 + [anywhere, vmem],
        out_specs=[vmem, vmem],
        scratch_shapes=[
            pltpu.VMEM((frames, 128), half),
            pltpu.VMEM((8, width), single),
            pltpu.VMEM((HALF + frames + after, 128), half),
            pltpu.VMEM((rows + 32, 128), single),
            pltpu.VMEM((n, 16, part), single),
            pltpu.VMEM((128, 4 * channels), single),
            pltpu.VMEM((rows + 16, 4 * channels), single),
            pltpu.VMEM((rows + 16, 4 * channels), half),
            pltpu.VMEM((rows + 16, channels), single),
            pltpu.VMEM((rows, channels), half),
            pltpu.VMEM((2, n, 3 * channels, part), half),
            pltpu.VMEM((2, 3 * channels, channels), half),
            pltpu.VMEM((2, channels), single),
            pltpu.VMEM((n, 2, channels), single),
            pltpu.VMEM((shards, 2, channels), single),
            pltpu.VMEM((rows, channels), half),
            pltpu.VMEM((n * rows, channels), half),
            pltpu.VMEM((groups, PHASES * GW, SPAN * GW), half),
            pltpu.VMEM((n * rows + 64, width), single),
            pltpu.VMEM((length + 64, 2 * GW), single),
            pltpu.VMEM((length + 16, SPAN // 2 * GW), half),
            pltpu.VMEM((length, PHASES * GW), single),
            pltpu.VMEM((frames, width), single),
            pltpu.VMEM((n, 2, frames), single),
            dma((2,)),
            dma((2,)),
            dma((2,)),
            dma((n,)),
            dma((n,)),
            dma((2, n // 2)),
            dma((2, n // 2)),
            dma((2, n // 2, recs)),
            dma((2, n // 2, recs)),
            dma((2, n // 2, recs)),
            dma((2, n // 2, recs)),
            dma((n,)),
            dma((n,)),
            dma((shards,)),
            dma((shards,)),
            dma((groups, PHASES)),
            dma((n // 2,)),
            dma((n // 2,)),
            dma((n // 2,)),
            dma((n // 2,)),
            dma((n,)),
            dma((n,)),
        ],
        compiler_params=pltpu.CompilerParams(
            collective_id=0, has_side_effects=True, vmem_limit_bytes=56 * 1024 * 1024
        ),
        name="encoder",
    )(
        waveform,
        first_weight,
        instance_gain,
        instance_bias,
        second_weight,
        third_weight,
        feature_gain,
        feature_bias,
        project_weight,
        project_bias,
        position_weight,
        position_bias,
    )


def local(
    waveform,
    first_weight,
    instance_gain,
    instance_bias,
    second_weight,
    third_weight,
    feature_gain,
    feature_bias,
    project_weight,
    project_bias,
    position_weight,
    position_bias,
    final_gain,
    final_bias,
):
    n = lax.axis_size("chan")
    shards = lax.axis_size("tm")
    channels, part = second_weight.shape[1:]
    width = project_weight.shape[1]
    summed, norm = encoder(
        waveform.reshape(-1, 20),
        first_weight,
        instance_gain[None],
        instance_bias[None],
        second_weight.reshape(3 * channels, part),
        third_weight.reshape(3 * channels, part),
        feature_gain[None],
        feature_bias[None],
        project_weight,
        project_bias[None],
        position_weight,
        position_bias[None],
        n,
        shards,
        width * n,
    )
    encoded = (summed - norm[0:1]) * norm[1:2] * final_gain[:, None] + final_bias[:, None]
    return encoded.astype(jnp.bfloat16)


def solution(mesh):
    return jax.shard_map(
        local,
        mesh=mesh,
        in_specs=(
            P(("rec", "tm")),
            P(None, "chan"),
            P("chan"),
            P("chan"),
            P(None, None, "chan"),
            P(None, None, "chan"),
            P(),
            P(),
            P(None, "chan"),
            P(),
            P("chan", None),
            P("chan"),
            P("chan"),
            P("chan"),
        ),
        out_specs=P("chan", ("rec", "tm")),
        check_vma=False,
    )
```

```python
import functools

import jax
import jax.numpy as jnp
from jax import lax
from jax.experimental import pallas as pl
from jax.experimental.pallas import tpu as pltpu
from jax.sharding import PartitionSpec as P

K = 128
GW = 64
HALF = K // 2
SPAN = 32
PHASES = K // SPAN
MESH = pl.DeviceIdType.MESH
NT = (((1,), (1,)), ((), ()))


def gelu_exact(values):
    return 0.5 * values * (1.0 + lax.erf(values * 0.7071067811865476))


def rows_per_device(frames, count):
    return -(-(frames + K) // (16 * count)) * 16


def encoder_kernel(
    n,
    shards,
    frames,
    rows,
    model_width,
    wave,
    first_weight,
    instance_gain,
    instance_bias,
    second_weight,
    third_weight,
    feature_gain,
    feature_bias,
    project_weight,
    project_bias,
    position_weight,
    position_bias,
    summed,
    norm,
    waveform,
    params,
    samples,
    sample32,
    smalls,
    band32,
    conv,
    first,
    shift32,
    second,
    slots,
    full,
    own_stats,
    chan_stats,
    tm_stats,
    normed,
    gathered,
    taps,
    x32,
    x2,
    window,
    partial,
    positional,
    stats,
    own_sem,
    halo_send,
    halo_recv,
    small_send,
    small_recv,
    weight_send,
    weight_recv,
    weight_pair_send,
    weight_pair_recv,
    rec_send,
    rec_recv,
    moment_send,
    moment_recv,
    total_send,
    total_recv,
    taps_sem,
    send_sem,
    recv_sem,
    pair_send,
    pair_recv,
    stat_send,
    stat_recv,
):
    me = lax.axis_index("chan")
    shard = lax.axis_index("tm")
    rec = lax.axis_index("rec")
    recs = lax.axis_size("rec")
    chips = n // 2
    chip, core = me // 2, lax.rem(me, 2)
    pair = chip * 2 + 1 - core
    width = summed.shape[0]
    groups = width // GW
    channels = feature_gain.shape[1]
    part = channels // n
    after = samples.shape[0] - HALF - frames
    sent = []

    def send(source, target, send_at, recv_at, **device):
        copy = pltpu.make_async_remote_copy(
            src_ref=source,
            dst_ref=target,
            send_sem=send_at,
            recv_sem=recv_at,
            device_id=device,
            device_id_type=MESH,
        )
        copy.start()
        sent.append(copy)
        return copy

    own_copies = []
    for index, weight in enumerate((second_weight, third_weight)):
        copy = pltpu.make_async_copy(weight, slots.at[index, me], own_sem.at[index])
        copy.start()
        own_copies.append(copy)

    barrier = pltpu.get_barrier_semaphore()
    for step in range(1, n):
        pl.semaphore_signal(
            barrier, inc=1, device_id={"chan": lax.rem(me + step, n)}, device_id_type=MESH
        )
    for step in range(1, shards):
        pl.semaphore_signal(
            barrier, inc=1, device_id={"tm": lax.rem(shard + step, shards)}, device_id_type=MESH
        )
    for step in range(1, recs):
        pl.semaphore_signal(
            barrier, inc=1, device_id={"rec": lax.rem(rec + step, recs)}, device_id_type=MESH
        )
    waveform[...] = jnp.zeros_like(waveform)
    waveform[:, 0:20] = wave[...]
    smalls[me] = jnp.concatenate(
        [
            first_weight[...].astype(jnp.float32),
            instance_gain[...],
            instance_bias[...],
            jnp.zeros((4, part), jnp.float32),
        ],
        axis=0,
    )
    pl.semaphore_wait(barrier, n + shards + recs - 3)

    following = send(
        waveform.at[pl.ds(0, after), :],
        samples.at[pl.ds(HALF + frames, after), :],
        halo_send.at[0],
        halo_recv.at[0],
        tm=lax.rem(shard + shards - 1, shards),
    )
    leading = send(
        waveform.at[pl.ds(frames - HALF, HALF), :],
        samples.at[pl.ds(0, HALF), :],
        halo_send.at[1],
        halo_recv.at[1],
        tm=lax.rem(shard + 1, shards),
    )
    small_copies = [
        send(
            smalls.at[me],
            smalls.at[me],
            small_send.at[step],
            small_recv.at[step],
            chan=lax.rem(me + step, n),
        )
        for step in range(1, n)
    ]
    weight_chip, weight_pair, weight_rec = [], [], [[], []]
    depth = 3 * channels // recs

    def share(owner):
        return pl.ds(pl.multiple_of(owner * depth, 16), depth)

    for index, weight in enumerate((second_weight, third_weight)):
        weight_chip.append(
            [
                send(
                    weight.at[share(rec), :],
                    slots.at[index, me, share(rec), :],
                    weight_send.at[index, step],
                    weight_recv.at[index, step],
                    chan=lax.rem(chip + step, chips) * 2 + core,
                )
                for step in range(1, chips)
            ]
        )
        weight_pair.append(
            [
                send(
                    weight,
                    slots.at[index, me],
                    weight_pair_send.at[index, 0, 0],
                    weight_pair_recv.at[index, 0, 0],
                    chan=pair,
                )
            ]
        )

    def forward_chip(index):
        for step in range(1, chips):
            other = lax.rem(chip + chips - step, chips) * 2 + core
            piece = slots.at[index, other, share(rec), :]
            weight_chip[index][step - 1].wait_recv()
            for turn in range(1, recs):
                weight_rec[index].append(
                    send(
                        piece,
                        piece,
                        rec_send.at[index, step, turn],
                        rec_recv.at[index, step, turn],
                        rec=lax.rem(rec + turn, recs),
                    )
                )
            weight_pair[index].append(
                send(
                    piece,
                    piece,
                    weight_pair_send.at[index, step, 0],
                    weight_pair_recv.at[index, step, 0],
                    chan=pair,
                )
            )

    def forward_rec(index):
        arrivals = iter(weight_rec[index])
        for step in range(1, chips):
            other = lax.rem(chip + chips - step, chips) * 2 + core
            for turn in range(1, recs):
                piece = slots.at[index, other, share(lax.rem(rec + recs - turn, recs)), :]
                next(arrivals).wait_recv()
                weight_pair[index].append(
                    send(
                        piece,
                        piece,
                        weight_pair_send.at[index, step, turn],
                        weight_pair_recv.at[index, step, turn],
                        chan=pair,
                    )
                )

    def assemble_weight(index):
        own_copies[index].wait()
        for copy in weight_pair[index]:
            copy.wait_recv()
        for source in range(n):
            full[index, :, source * part : (source + 1) * part] = slots[index, source]

    tap_copies = []
    for g in range(groups):
        for p in range(PHASES):
            copy = pltpu.make_async_copy(
                position_weight.at[pl.ds(g * GW, GW), pl.ds(p * SPAN * GW, SPAN * GW)],
                taps.at[g, pl.ds(p * GW, GW), :],
                taps_sem.at[g, p],
            )
            copy.start()
            tap_copies.append(copy)

    samples[HALF : HALF + frames, :] = waveform[...]
    chosen = project_bias[:, 0:width]
    for source in range(1, n):
        chosen = jnp.where(me == source, project_bias[:, source * width : (source + 1) * width], chosen)
    params[...] = jnp.concatenate(
        [chosen, position_bias[...], jnp.zeros((6, width), jnp.float32)], axis=0
    )
    following.wait_recv()
    leading.wait_recv()
    for copy in small_copies:
        copy.wait_recv()

    extra = rows + 16
    place = me * rows - HALF + lax.broadcasted_iota(jnp.int32, (rows + 32, 1), 0)
    inside = (shard * frames + place >= 0) & (shard * frames + place < shards * frames)
    row = lax.broadcasted_iota(jnp.int32, (extra, 1), 0)
    counted = (place[:extra] >= 0) & (place[:extra] < frames) & (row < rows)
    held = samples[pl.ds(pl.multiple_of(me * rows, 16), rows + 32), :].astype(jnp.float32)
    sample32[...] = jnp.where(inside, held, 0.0)
    patches = (
        sample32[0:extra, :] + pltpu.roll(sample32[1 : extra + 1, :], 20, axis=1)
    ).astype(jnp.bfloat16)

    band32[...] = jnp.zeros_like(band32)
    for f in range(4):
        for source in range(n):
            at = f * channels + source * part
            band32[5 * f : 5 * f + 10, at : at + part] = smalls[source, 0:10, :]
    moments = jnp.zeros((2, channels), jnp.float32)
    for f in range(4):
        lanes = slice(f * channels, (f + 1) * channels)
        values = jnp.dot(
            patches, band32[:, lanes].astype(jnp.bfloat16), preferred_element_type=jnp.float32
        )
        conv[:, lanes] = values
        kept = jnp.where(counted, values, 0.0)
        moments = moments + jnp.concatenate(
            [jnp.sum(kept, axis=0, keepdims=True), jnp.sum(kept * kept, axis=0, keepdims=True)],
            axis=0,
        )
    own_stats[...] = moments
    chan_stats[me] = moments
    moment_copies = [
        send(
            own_stats,
            chan_stats.at[me],
            moment_send.at[step],
            moment_recv.at[step],
            chan=lax.rem(me + step, n),
        )
        for step in range(1, n)
    ]
    gain = jnp.concatenate([smalls[source, 10:11, :] for source in range(n)], axis=1)
    offset = jnp.concatenate([smalls[source, 11:12, :] for source in range(n)], axis=1)
    forward_chip(0)
    for copy in moment_copies:
        copy.wait_recv()
    moments = chan_stats[0]
    for index in range(1, n):
        moments = moments + chan_stats[index]
    tm_stats[shard] = moments
    total_copies = [
        send(
            tm_stats.at[shard],
            tm_stats.at[shard],
            total_send.at[step],
            total_recv.at[step],
            tm=lax.rem(shard + step, shards),
        )
        for step in range(1, shards)
    ]
    x32[n * rows :, :] = jnp.zeros_like(x32[n * rows :, :])
    x2[...] = jnp.zeros_like(x2)
    for copy in total_copies:
        copy.wait_recv()
    moments = tm_stats[0]
    for index in range(1, shards):
        moments = moments + tm_stats[index]
    moments = moments / (4 * frames * shards)
    mean = moments[0:1]
    scale = lax.rsqrt(moments[1:2] - mean * mean + 1e-05)

    forward_chip(1)
    forward_rec(0)
    for f in range(4):
        lanes = slice(f * channels, (f + 1) * channels)
        values = gelu_exact((conv[:, lanes] - mean) * scale * gain + offset)
        values = jnp.where(inside[:extra], values, 0.0).astype(jnp.bfloat16)
        first[:, lanes] = values
        if f == 0:
            shift32[...] = values.astype(jnp.float32)

    def dot(a, b):
        return jnp.dot(a, b, preferred_element_type=jnp.float32)

    c = channels
    forward_rec(1)
    assemble_weight(0)
    second[0:rows, :] = gelu_exact(
        dot(first[0:rows, 2 * c :], full[0, 0 : 2 * c, :])
        + dot(shift32[1 : rows + 1, :].astype(jnp.bfloat16), full[0, 2 * c :, :])
    ).astype(jnp.bfloat16)
    even = gelu_exact(dot(first[:, 0 : 3 * c], full[0])).astype(jnp.bfloat16)
    shift32[...] = even.astype(jnp.float32)
    assemble_weight(1)
    def block(index):
        return gathered.at[pl.ds(pl.multiple_of(index * rows, 16), rows), :]

    pieces = 2 if rows % 32 == 0 else 1
    size = rows // pieces

    def piece(index, h):
        return gathered.at[pl.ds(pl.multiple_of(index * rows + h * size, 16), size), :]

    chip_copies, first_pair = [], []
    for h in range(pieces):
        own = slice(h * size, (h + 1) * size)
        third = gelu_exact(
            dot(even[own], full[1, 0:c, :])
            + dot(second[own, :], full[1, c : 2 * c, :])
            + dot(
                shift32[h * size + 1 : (h + 1) * size + 1, :].astype(jnp.bfloat16),
                full[1, 2 * c :, :],
            )
        )
        third = third.astype(jnp.bfloat16).astype(jnp.float32)
        centred = third - jnp.mean(third, axis=1, keepdims=True)
        spread = jnp.mean(centred * centred, axis=1, keepdims=True)
        normed[own, :] = (
            centred * lax.rsqrt(spread + 1e-05) * feature_gain[...] + feature_bias[...]
        ).astype(jnp.bfloat16)
        for step in range(1, chips):
            chip_copies.append(
                send(
                    normed.at[pl.ds(h * size, size), :],
                    piece(me, h),
                    send_sem.at[step, h],
                    recv_sem.at[step, h],
                    chan=lax.rem(chip + step, chips) * 2 + core,
                )
            )
        first_pair.append(
            send(
                normed.at[pl.ds(h * size, size), :],
                piece(me, h),
                pair_send.at[0, h],
                pair_recv.at[0, h],
                chan=pair,
            )
        )

    def project(index, source):
        values = jnp.dot(source[...], project_weight[...], preferred_element_type=jnp.float32)
        values = (values + params[0:1, :]).astype(jnp.bfloat16).astype(jnp.float32)
        frame = (
            shard * frames
            - HALF
            + index * rows
            + lax.broadcasted_iota(jnp.int32, (rows, 1), 0)
        )
        inside = (frame >= 0) & (frame < shards * frames)
        x32[pl.ds(pl.multiple_of(index * rows, 8), rows), :] = jnp.where(inside, values, 0.0)

    project(me, normed)
    for copy in first_pair:
        copy.wait_recv()
    project(pair, block(pair))
    forwards = []
    for h in range(pieces):
        for step in range(1, chips):
            other = lax.rem(chip + chips - step, chips) * 2 + core
            chip_copies[h * (chips - 1) + step - 1].wait_recv()
            forwards.append(
                send(
                    piece(other, h),
                    piece(other, h),
                    pair_send.at[step, h],
                    pair_recv.at[step, h],
                    chan=pair,
                )
            )
    for step in range(1, chips):
        other = lax.rem(chip + chips - step, chips) * 2 + core
        project(other, block(other))
    for copy in forwards:
        copy.wait_recv()
    for step in range(1, chips):
        other = lax.rem(chip + chips - step, chips) * 2 + 1 - core
        project(other, block(other))

    length = frames + K
    chunk = length // 4
    for g in range(groups):
        lanes = slice(g * GW, (g + 1) * GW)
        x2[0:length, :] = jnp.concatenate(
            [x32[0:length, lanes], x32[1 : length + 1, lanes]], axis=1
        )
        for q in range(SPAN // 4):
            window[:, q * 2 * GW : (q + 1) * 2 * GW] = x2[
                2 * q : 2 * q + length + 16, :
            ].astype(jnp.bfloat16)
        for p in range(PHASES):
            tap_copies[g * PHASES + p].wait()
        middle = SPAN // 2 * GW

        @pl.loop(0, 4)
        def _(m):
            start = pl.multiple_of(m * chunk, 16)
            partial[pl.ds(start, chunk), :] = lax.dot_general(
                window[pl.ds(start, chunk), :],
                taps[g, :, 0:middle],
                NT,
                preferred_element_type=jnp.float32,
            ) + lax.dot_general(
                window[pl.ds(pl.multiple_of(start + 16, 16), chunk), :],
                taps[g, :, middle : 2 * middle],
                NT,
                preferred_element_type=jnp.float32,
            )

        total = partial[0:frames, 0:GW]
        for p in range(1, PHASES):
            total = total + partial[p * SPAN : p * SPAN + frames, p * GW : (p + 1) * GW]
        positional[:, lanes] = total

    tile = 128

    @pl.loop(0, frames // tile)
    def _(m):
        start = pl.multiple_of(m * tile, tile)
        values = x32[pl.ds(start + HALF, tile), :] + gelu_exact(
            positional[pl.ds(start, tile), :] + params[1:2, :]
        )
        turned = values.T
        summed[:, pl.ds(start, tile)] = turned
        stats[me, 0:1, pl.ds(start, tile)] = jnp.sum(turned, axis=0, keepdims=True)
        stats[me, 1:2, pl.ds(start, tile)] = jnp.sum(turned * turned, axis=0, keepdims=True)

    stat_copies = []
    for step in range(1, n):
        copy = pltpu.make_async_remote_copy(
            src_ref=stats.at[me],
            dst_ref=stats.at[me],
            send_sem=stat_send.at[step],
            recv_sem=stat_recv.at[step],
            device_id={"chan": lax.rem(me + step, n)},
            device_id_type=MESH,
        )
        copy.start()
        stat_copies.append(copy)
    for copy in stat_copies:
        copy.wait_recv()
    both = stats[0]
    for index in range(1, n):
        both = both + stats[index]
    mean = both[0:1] / model_width
    norm[0:1, :] = mean
    norm[1:2, :] = lax.rsqrt(both[1:2] / model_width - mean * mean + 1e-05)

    for copy in sent + stat_copies:
        copy.wait_send()


def encoder(
    waveform,
    first_weight,
    instance_gain,
    instance_bias,
    second_weight,
    third_weight,
    feature_gain,
    feature_bias,
    project_weight,
    project_bias,
    position_weight,
    position_bias,
    n,
    shards,
    model_width,
):
    frames = waveform.shape[0]
    rows = rows_per_device(frames, n)
    after = -(-(n * rows - HALF - frames + 32) // 16) * 16
    channels = feature_gain.shape[1]
    part = channels // n
    recs = lax.axis_size("rec")
    width = project_weight.shape[1]
    groups = width // GW
    length = frames + K
    vmem = pl.BlockSpec(memory_space=pltpu.VMEM)
    anywhere = pl.BlockSpec(memory_space=pl.ANY)
    dma = pltpu.SemaphoreType.DMA
    half = jnp.bfloat16
    single = jnp.float32
    return pl.pallas_call(
        functools.partial(encoder_kernel, n, shards, frames, rows, model_width),
        out_shape=[
            jax.ShapeDtypeStruct((width, frames), single),
            jax.ShapeDtypeStruct((2, frames), single),
        ],
        in_specs=[vmem] * 4 + [anywhere] * 2 + [vmem] * 4 + [anywhere, vmem],
        out_specs=[vmem, vmem],
        scratch_shapes=[
            pltpu.VMEM((frames, 128), half),
            pltpu.VMEM((8, width), single),
            pltpu.VMEM((HALF + frames + after, 128), half),
            pltpu.VMEM((rows + 32, 128), single),
            pltpu.VMEM((n, 16, part), single),
            pltpu.VMEM((128, 4 * channels), single),
            pltpu.VMEM((rows + 16, 4 * channels), single),
            pltpu.VMEM((rows + 16, 4 * channels), half),
            pltpu.VMEM((rows + 16, channels), single),
            pltpu.VMEM((rows, channels), half),
            pltpu.VMEM((2, n, 3 * channels, part), half),
            pltpu.VMEM((2, 3 * channels, channels), half),
            pltpu.VMEM((2, channels), single),
            pltpu.VMEM((n, 2, channels), single),
            pltpu.VMEM((shards, 2, channels), single),
            pltpu.VMEM((rows, channels), half),
            pltpu.VMEM((n * rows, channels), half),
            pltpu.VMEM((groups, PHASES * GW, SPAN * GW), half),
            pltpu.VMEM((n * rows + 64, width), single),
            pltpu.VMEM((length + 64, 2 * GW), single),
            pltpu.VMEM((length + 16, SPAN // 2 * GW), half),
            pltpu.VMEM((length, PHASES * GW), single),
            pltpu.VMEM((frames, width), single),
            pltpu.VMEM((n, 2, frames), single),
            dma((2,)),
            dma((2,)),
            dma((2,)),
            dma((n,)),
            dma((n,)),
            dma((2, n // 2)),
            dma((2, n // 2)),
            dma((2, n // 2, recs)),
            dma((2, n // 2, recs)),
            dma((2, n // 2, recs)),
            dma((2, n // 2, recs)),
            dma((n,)),
            dma((n,)),
            dma((shards,)),
            dma((shards,)),
            dma((groups, PHASES)),
            dma((n // 2, 2)),
            dma((n // 2, 2)),
            dma((n // 2, 2)),
            dma((n // 2, 2)),
            dma((n,)),
            dma((n,)),
        ],
        compiler_params=pltpu.CompilerParams(
            collective_id=0, has_side_effects=True, vmem_limit_bytes=56 * 1024 * 1024
        ),
        name="encoder",
    )(
        waveform,
        first_weight,
        instance_gain,
        instance_bias,
        second_weight,
        third_weight,
        feature_gain,
        feature_bias,
        project_weight,
        project_bias,
        position_weight,
        position_bias,
    )


def local(
    waveform,
    first_weight,
    instance_gain,
    instance_bias,
    second_weight,
    third_weight,
    feature_gain,
    feature_bias,
    project_weight,
    project_bias,
    position_weight,
    position_bias,
    final_gain,
    final_bias,
):
    n = lax.axis_size("chan")
    shards = lax.axis_size("tm")
    channels, part = second_weight.shape[1:]
    width = project_weight.shape[1]
    summed, norm = encoder(
        waveform.reshape(-1, 20),
        first_weight,
        instance_gain[None],
        instance_bias[None],
        second_weight.reshape(3 * channels, part),
        third_weight.reshape(3 * channels, part),
        feature_gain[None],
        feature_bias[None],
        project_weight,
        project_bias[None],
        position_weight,
        position_bias[None],
        n,
        shards,
        width * n,
    )
    encoded = (summed - norm[0:1]) * norm[1:2] * final_gain[:, None] + final_bias[:, None]
    return encoded.astype(jnp.bfloat16)


def solution(mesh):
    return jax.shard_map(
        local,
        mesh=mesh,
        in_specs=(
            P(("rec", "tm")),
            P(None, "chan"),
            P("chan"),
            P("chan"),
            P(None, None, "chan"),
            P(None, None, "chan"),
            P(),
            P(),
            P(None, "chan"),
            P(),
            P("chan", None),
            P("chan"),
            P("chan"),
            P("chan"),
        ),
        out_specs=P("chan", ("rec", "tm")),
        check_vma=False,
    )
```
